512 devices in a mesh: ctx: 64 (over z, x_lo, core), head: 8 (over y, x_hi).
Axes of the slice: x: 4 (x_hi: 2, x_lo: 2; x = x_hi * 2 + x_lo), y: 4, z: 16, core: 2. Of those that a mesh axis runs over, the one named last changes fastest.
Arguments:
- queries: bfloat16 [12480, 3072], P('ctx', 'head'), may hold values from -6 to 6
- keys: bfloat16 [12480, 3072], P('ctx', 'head'), may hold values from -6 to 6
- values: bfloat16 [12480, 3072], P('ctx', 'head'), may hold values from -6 to 6
- rates: float32 [12480, 24], P('ctx', 'head'), may hold values from 0.1 to 1
- frame_update: int32 [64], P('ctx'), may hold values 0 or 1
- fast_weights: float32 [3, 24, 512, 128], P(None, 'head', 'ctx'), may hold values from -2 to 2
- gain: float32 [3072], P('head'), may hold values from 0.5 to 1.5
Outputs:
- block_out: bfloat16 [12480, 3072], P('ctx', 'head')
- new_weights: float32 [3, 24, 512, 128], P(None, 'head', 'ctx')
The draws below stay inside these ranges and needn't reach their ends.
All inputs are finite; a program needn't handle non-finite values. No bound on the sum of `frame_update` on one device may be relied on, other than what follows from the above.
Results may differ from the reference program's by a relative error of at most 0.0071.
Values may be sent and summed in bfloat16 or wider, within the bound.
A program may use at most 64 MiB of HBM per device.

```python
import math
import jax
import jax.numpy as jnp
from jax import lax

HD = 128
HID = 512
FRAME = 195
NS_STEPS = 5
HEADS = 24
FRAMES = 64
TOKENS = 12480


def draw_queries(key, part):
    key = jax.random.fold_in(key, 5)
    base = jnp.clip(jax.random.normal(key, (TOKENS, HEADS * HD), jnp.float32), -6.0, 6.0)
    return base.astype(jnp.bfloat16)


def draw_keys(key, part):
    key = jax.random.fold_in(key, 7)
    base = jnp.clip(jax.random.normal(key, (TOKENS, HEADS * HD), jnp.float32), -6.0, 6.0)
    return base.astype(jnp.bfloat16)


def draw_fast_weights(key, part):
    key = jax.random.fold_in(key, 9)
    noise_key = jax.random.fold_in(key, 0)
    base = jnp.clip(jax.random.normal(noise_key, (3, HEADS, HID, HD), jnp.float32), -5.0, 5.0)
    rise = 3.0 ** (jnp.arange(HEADS, dtype=jnp.float32) / max(HEADS - 1, 1))
    ones_row = jnp.ones((HEADS,), jnp.float32)
    scale = jnp.stack([ones_row * HD ** (-0.5), ones_row * HD ** (-0.5), rise * HID ** (-0.5)])
    return jnp.clip(base * scale[:, :, None, None], -2.0, 2.0)


def with_ends(drawn, rng, smallest, top_value):
    index_at = [jax.random.randint(jax.random.fold_in(rng, axis), (), 0, length) for axis, length in enumerate(drawn.shape)]
    widest = drawn.shape.index(max(drawn.shape))
    beside = index_at[:widest] + [(index_at[widest] + 1) % drawn.shape[widest]] + index_at[widest + 1:]
    return drawn.at[tuple(index_at)].set(smallest).at[tuple(beside)].set(top_value)


def level_of(key, shape, pieces, least, high):
    def one(dim, shards_of):
        draws = jax.random.uniform(jax.random.fold_in(jax.random.fold_in(key, 6), dim), (shards_of,), jnp.float32, least / len(pieces), high / len(pieces))
        return jnp.repeat(jnp.exp(draws), shape[dim] // shards_of).reshape((-1,) + (1,) * (len(shape) - dim - 1))

    loudness = one(*pieces[0])
    for cut in pieces[1:]:
        loudness = loudness * one(*cut)
    return loudness


def gaussian(key, extent, scale, most, shards=(), held_as=jnp.bfloat16):
    entries = scale * jax.random.normal(key, extent, jnp.float32)
    if shards:
        entries = entries * level_of(key, extent, shards, -0.22, 0.18)
    return jnp.clip(entries, -most, most).astype(held_as)


def setup_inputs(seed: int = 0) -> dict:
    arg_keys = jax.random.split(jax.random.key(seed), 8)
    queries = draw_queries(jax.random.fold_in(arg_keys[7], 71), 0)
    keys = draw_keys(jax.random.fold_in(arg_keys[7], 71), 0)
    values = gaussian(arg_keys[2], (TOKENS, HEADS * HD), 1.0, 6.0, ((0, 64), (1, 8)))
    rates = jnp.clip(jnp.exp(math.log(1.0) - 2.3025851 * jax.random.uniform(arg_keys[3], (TOKENS, HEADS), jnp.float32) ** level_of(arg_keys[3], (TOKENS, HEADS), ((0, 64), (1, 8)), -0.2, 0.2)), 0.1, 1.0)
    frame_update = with_ends((jax.random.randint(arg_keys[4], (FRAMES,), 0, 4) < 3).astype(jnp.int32), jax.random.fold_in(arg_keys[4], 1), 0, 1)
    fast_weights = draw_fast_weights(jax.random.fold_in(arg_keys[7], 71), 0)
    gain = jnp.clip(1.0 + 0.1 * jax.random.normal(arg_keys[6], (HEADS * HD,), jnp.float32), 0.5, 1.5)
    return {"queries": queries, "keys": keys, "values": values, "rates": rates, "frame_update": frame_update, "fast_weights": fast_weights, "gain": gain}


epsilon = 1e-06
quintic_a = 3.4445
quintic_b = -4.775
quintic_c = 2.0315
highest = lax.Precision.HIGHEST

def frame_attention(queries, keys, values):
    frame_count = queries.shape[0] // FRAME
    head_count = queries.shape[1] // HD
    shaped_q = queries.reshape(frame_count, FRAME, head_count, HD)
    shaped_k = keys.reshape(frame_count, FRAME, head_count, HD)
    shaped_v = values.reshape(frame_count, FRAME, head_count, HD)
    before_k = jnp.concatenate([jnp.zeros_like(shaped_k[:1]), shaped_k[:-1]], axis=0)
    before_v = jnp.concatenate([jnp.zeros_like(shaped_v[:1]), shaped_v[:-1]], axis=0)
    frame_ids = jnp.arange(frame_count, dtype=jnp.int32)

    def one_frame(items):
        query_block, key_block, value_block, key_before, value_before, frame_id = items
        key_window = jnp.concatenate([key_before, key_block], axis=0).astype(jnp.float32)
        value_window = jnp.concatenate([value_before, value_block], axis=0).astype(jnp.float32)
        scores = jnp.einsum('qhd,khd->hqk', query_block.astype(jnp.float32), key_window) * HD ** (-0.5)
        valid = jnp.concatenate([jnp.full((FRAME,), frame_id > 0), jnp.ones((FRAME,), jnp.bool_)])
        scores = jnp.where(valid[None, None, :], scores, -1e+30)
        row_max = lax.optimization_barrier(jnp.max(scores, axis=2, keepdims=True))
        weights_exp = jnp.exp(scores - row_max)
        probs = (weights_exp / lax.optimization_barrier(jnp.sum(weights_exp, axis=2, keepdims=True))).astype(jnp.bfloat16)
        attended = jnp.einsum('hqk,khd->qhd', probs.astype(jnp.float32), value_window)
        return attended.reshape(FRAME, head_count * HD)
    blocks = lax.map(one_frame, (shaped_q, shaped_k, shaped_v, before_k, before_v, frame_ids))
    return blocks.reshape(frame_count * FRAME, head_count * HD)

def head_terms(items):
    query_h, key_h, value_h, rate_h, weights_h = items
    proj_one = jnp.dot(query_h, weights_h[0].T, preferred_element_type=jnp.float32)
    proj_three = jnp.dot(query_h, weights_h[1].T, preferred_element_type=jnp.float32)
    hidden_q = (jax.nn.silu(proj_one) * proj_three).astype(jnp.bfloat16)
    fast_out = jnp.dot(hidden_q, weights_h[2], preferred_element_type=jnp.float32)
    pre_one = jnp.dot(key_h, weights_h[0].T, preferred_element_type=jnp.float32)
    pre_three = jnp.dot(key_h, weights_h[1].T, preferred_element_type=jnp.float32)
    gate_act = jax.nn.silu(pre_one)
    act = (gate_act * pre_three).astype(jnp.bfloat16)
    target = (rate_h[:, None] * value_h.astype(jnp.float32)).astype(jnp.bfloat16)
    back = jnp.dot(target, weights_h[2].T, preferred_element_type=jnp.float32)
    sigmoid_pre = jax.nn.sigmoid(pre_one)
    delta_one = (back * pre_three * sigmoid_pre * (1.0 + pre_one * (1.0 - sigmoid_pre))).astype(jnp.bfloat16)
    delta_three = (back * gate_act).astype(jnp.bfloat16)
    grad_one = jnp.dot(delta_one.T, key_h, preferred_element_type=jnp.float32)
    grad_three = jnp.dot(delta_three.T, key_h, preferred_element_type=jnp.float32)
    grad_two = jnp.dot(act.T, target, preferred_element_type=jnp.float32)
    return (fast_out, jnp.stack([grad_one, grad_three, grad_two]))

def reference(queries, keys, values, rates, frame_update, fast_weights, gain):
    head_count = queries.shape[1] // HD
    tokens_all = queries.shape[0]
    low_weights = fast_weights.astype(jnp.bfloat16)
    attended = frame_attention(queries, keys, values)
    keep_token = jnp.repeat(frame_update.astype(jnp.float32), FRAME)
    split_q = queries.reshape(tokens_all, head_count, HD).transpose(1, 0, 2)
    split_k = keys.reshape(tokens_all, head_count, HD).transpose(1, 0, 2)
    split_v = values.reshape(tokens_all, head_count, HD).transpose(1, 0, 2)
    rate_heads = (rates * keep_token[:, None]).T
    fast_out, grads = lax.map(head_terms, (split_q, split_k, split_v, rate_heads, low_weights.transpose(1, 0, 2, 3)))
    fast_out = fast_out.transpose(1, 0, 2).reshape(tokens_all, head_count * HD)
    spread = lax.optimization_barrier(jnp.mean(fast_out * fast_out, axis=1, keepdims=True))
    block_out = (attended + fast_out * gain[None, :] * lax.rsqrt(spread + epsilon)).astype(jnp.bfloat16)
    grads = grads.transpose(1, 0, 2, 3)
    squares = lax.optimization_barrier(jnp.sum(grads * grads, axis=(2, 3), keepdims=True))
    ortho = grads * lax.rsqrt(squares + epsilon)
    for section_index in range(NS_STEPS):
        gram_matrix = jnp.einsum('mhjd,mhje->mhde', ortho, ortho, precision=highest)
        square_gram = jnp.einsum('mhde,mhef->mhdf', gram_matrix, gram_matrix, precision=highest)
        mix_matrix = quintic_b * gram_matrix + quintic_c * square_gram
        ortho = quintic_a * ortho + jnp.einsum('mhjd,mhde->mhje', ortho, mix_matrix, precision=highest)
    summed = fast_weights + ortho
    old_norm = jnp.sqrt(lax.optimization_barrier(jnp.sum(fast_weights * fast_weights, axis=3, keepdims=True)))
    new_weights = summed * old_norm * lax.rsqrt(lax.optimization_barrier(jnp.sum(summed * summed, axis=3, keepdims=True)) + epsilon)
    return (block_out, new_weights)
```

```python
import jax
import jax.numpy as jnp
from jax import lax
from jax.experimental import pallas as pl
from jax.experimental.pallas import tpu as pltpu
from jax.sharding import PartitionSpec as P

HD = 128
FRAME = 195
PAD = 208
NS_STEPS = 5
NZ = 16
OWNERS = (0, 5, 11, 2, 7, 12, 4, 9, 14)
MESH = pl.DeviceIdType.MESH
BF = jnp.bfloat16
F32 = jnp.float32

epsilon = 1e-06
quintic_a = 3.4445
quintic_b = -4.775
quintic_c = 2.0315


def dot(a, b, dims, precision=None):
    return lax.dot_general(a, b, (dims, ((), ())), precision=precision, preferred_element_type=F32)


def exact(a, b, dims=((1,), (0,))):
    return dot(a, b, dims, lax.Precision.HIGHEST)


def ctx_id(z, x, k):
    return (z * 2 + x) * 2 + k


def padded(value):
    return jnp.concatenate([value, jnp.zeros((PAD - FRAME, value.shape[1]), value.dtype)], axis=0)


def kernel(
    q_ref, k_ref, v_ref, r_ref, fu_ref, fw_ref, gain_ref,
    bo_ref, nw_ref,
    wag_a, wag_b, wag_c, kt, wfull, gbuf, grecv, kv, halo, squares, grams, osend, orecv,
    ag_send, ag_recv, kt_send, kt_recv, wf_send, wf_recv, g_send, g_recv,
    halo_send, halo_recv, sq_send, sq_recv, gram_send, gram_recv, o_send, o_recv,
):
    c = lax.axis_index("ctx")
    hd = lax.axis_index("head")
    z, x, k = c // 4, lax.rem(c // 2, 2), lax.rem(c, 2)
    quarter = lax.rem(c, 4)
    peers = [ctx_id(z, x, 1 - k), ctx_id(z, 1 - x, k), ctx_id(z, 1 - x, 1 - k)]
    after, before = lax.rem(c + 1, 64), lax.rem(c + 63, 64)

    barrier = pltpu.get_barrier_semaphore()

    def greet_line(step, carry):
        there = ctx_id(lax.rem(z + step, NZ), x, k)
        pl.semaphore_signal(barrier, inc=1, device_id={"ctx": there}, device_id_type=MESH)
        return carry

    def greet_head(step, carry):
        pl.semaphore_signal(
            barrier, inc=1, device_id={"head": lax.rem(hd + step, 8)}, device_id_type=MESH
        )
        return carry

    lax.fori_loop(1, NZ, greet_line, 0)
    lax.fori_loop(1, 8, greet_head, 0)
    for peer in peers:
        pl.semaphore_signal(barrier, inc=1, device_id={"ctx": peer}, device_id_type=MESH)
    last, first = quarter == 3, quarter == 0

    @pl.when(last)
    def _():
        pl.semaphore_signal(barrier, inc=1, device_id={"ctx": after}, device_id_type=MESH)

    @pl.when(first)
    def _():
        pl.semaphore_signal(barrier, inc=1, device_id={"ctx": before}, device_id_type=MESH)

    def block(index):
        return fw_ref[index % 3, index // 3]

    def pair(index):
        second = block(index + 1) if index < 8 else jnp.zeros((8, HD), F32)
        return jnp.concatenate([block(index), second], axis=0).astype(BF)

    wag_a[z, 0:16] = pair(0)
    wag_a[z, 16:32] = pair(2)
    wag_b[z] = pair(4)
    wag_c[z, 0:16] = pair(6)
    wag_c[z, 16:32] = pair(8)
    groups = (wag_a, wag_b, wag_c)

    keep = fu_ref[0].astype(F32)
    for h in range(3):
        lanes = slice(h * HD, h * HD + HD)
        key_h, value_h = k_ref[:, lanes], v_ref[:, lanes]
        target = ((r_ref[:, h : h + 1] * keep) * value_h.astype(F32)).astype(BF)
        key_h = padded(key_h)
        kt[h, quarter, 0] = key_h
        kt[h, quarter, 1] = padded(target)
        kv[0, h] = key_h
        kv[1, h] = padded(value_h)

    pl.semaphore_wait(barrier, 25 + last.astype(jnp.int32) + first.astype(jnp.int32))

    def remote(src, dst, send, recv, device):
        return pltpu.make_async_remote_copy(
            src_ref=src, dst_ref=dst, send_sem=send, recv_sem=recv, device_id=device, device_id_type=MESH
        )

    def bytes_of(ref, sem):
        pltpu.make_async_copy(ref, ref, sem).wait()

    for g in range(3):
        def send_group(step, carry, g=g):
            there = ctx_id(lax.rem(z + step, NZ), x, k)
            remote(groups[g].at[z], groups[g].at[z], ag_send.at[g], ag_recv.at[g], {"ctx": there}).start()
            return carry

        lax.fori_loop(1, NZ, send_group, 0)
        for peer in peers:
            remote(
                kt.at[g, quarter], kt.at[g, quarter], kt_send.at[g], kt_recv.at[g], {"ctx": peer}
            ).start()

    def weight_block(index):
        group, tile = ((0, 0), (0, 1), (1, 0), (2, 0), (2, 1))[index // 2]
        both = groups[group][:, tile * 16 : tile * 16 + 16, :].astype(F32)
        half = both.reshape(NZ, 2, 8, HD)[:, index % 2]
        return half.reshape(HD, HD).astype(BF)

    for h in range(3):
        if h == 0:
            bytes_of(wag_a.at[pl.ds(0, 15)], ag_recv.at[0])
        elif h == 1:
            bytes_of(wag_b.at[pl.ds(0, 15)], ag_recv.at[1])
        else:
            bytes_of(wag_c.at[pl.ds(0, 15)], ag_recv.at[2])
        for m in range(3):
            wfull[h, quarter, m * HD : m * HD + HD] = weight_block(h * 3 + m)
        for peer in peers:
            remote(
                wfull.at[h, quarter], wfull.at[h, quarter], wf_send.at[h], wf_recv.at[h], {"ctx": peer}
            ).start()
        bytes_of(kt.at[h, pl.ds(0, 3)], kt_recv.at[h])
        w13 = wfull[h, quarter, 0 : 2 * HD]
        w2 = wfull[h, quarter, 2 * HD : 3 * HD]
        grad13 = jnp.zeros((2 * HD, HD), F32)
        grad2 = jnp.zeros((HD, HD), F32)
        for j in range(4):
            key_j, target_j = kt[h, j, 0], kt[h, j, 1]
            pre = dot(key_j, w13, ((1,), (1,)))
            pre_one, pre_three = pre[:, :HD], pre[:, HD:]
            back = dot(target_j, w2, ((1,), (1,)))
            sig = jax.nn.sigmoid(pre_one)
            gate = pre_one * sig
            act = (gate * pre_three).astype(BF)
            delta_one = (back * pre_three * sig * (1.0 + pre_one * (1.0 - sig))).astype(BF)
            delta_three = (back * gate).astype(BF)
            delta = jnp.concatenate([delta_one, delta_three], axis=1)
            grad13 = grad13 + dot(delta, key_j, ((0,), (0,)))
            grad2 = grad2 + dot(act, target_j, ((0,), (0,)))
        for m, grad in enumerate((grad13[:HD], grad13[HD:], grad2)):
            index = h * 3 + m
            owner = OWNERS[index]
            gbuf[index] = grad.astype(BF)

            @pl.when(z != owner)
            def _(index=index, owner=owner):
                remote(
                    gbuf.at[index], grecv.at[z], g_send.at[index], g_recv, {"ctx": ctx_id(owner, x, k)}
                ).start()

            @pl.when(z == owner)
            def _(grad=grad):
                grecv[z] = grad.astype(BF)

    remote(kv, halo, halo_send, halo_recv, {"ctx": after}).start()

    fast = []
    for h in range(3):
        bytes_of(wfull.at[h, pl.ds(0, 3)], wf_recv.at[h])
        query_h = padded(q_ref[:, h * HD : h * HD + HD])
        total = jnp.zeros((PAD, HD), F32)
        for j in range(4):
            proj = dot(query_h, wfull[h, j, 0 : 2 * HD], ((1,), (1,)))
            one, three = proj[:, :HD], proj[:, HD:]
            hidden = (one * jax.nn.sigmoid(one) * three).astype(BF)
            total = total + dot(hidden, wfull[h, j, 2 * HD : 3 * HD], ((1,), (0,)))
        fast.append(total)
    square_sum = fast[0] * fast[0] + fast[1] * fast[1] + fast[2] * fast[2]
    squares[hd] = exact(jnp.ones((8, HD), F32), square_sum, ((1,), (1,)))

    def send_squares(step, carry):
        there = lax.rem(hd + step, 8)
        remote(squares.at[hd], squares.at[hd], sq_send, sq_recv, {"head": there}).start()
        return carry

    lax.fori_loop(1, 8, send_squares, 0)

    is_owner = z == OWNERS[0]
    for owner in OWNERS[1:]:
        is_owner = jnp.logical_or(is_owner, z == owner)

    @pl.when(is_owner)
    def _():
        bytes_of(grecv.at[pl.ds(0, 15)], g_recv)
        grad = grecv[0].astype(F32)
        for j in range(1, NZ):
            grad = grad + grecv[j].astype(F32)
        grams[0] = exact(grad, grad, ((0,), (0,)))
        copy = remote(grams.at[0], grams.at[1], gram_send.at[0], gram_recv.at[0], {"ctx": peers[0]})
        copy.start()
        copy.wait()
        grams[2] = grams[0] + grams[1]
        copy = remote(grams.at[2], grams.at[3], gram_send.at[1], gram_recv.at[1], {"ctx": peers[1]})
        copy.start()
        copy.wait()
        gram = grams[2] + grams[3]
        rows = lax.broadcasted_iota(jnp.int32, (HD, HD), 0)
        columns = lax.broadcasted_iota(jnp.int32, (HD, HD), 1)
        eye = (rows == columns).astype(F32)
        norm = lax.rsqrt(jnp.sum(jnp.sum(gram * eye, axis=0, keepdims=True), axis=1, keepdims=True) + epsilon)
        gram = gram * (norm * norm)
        product = None
        for step in range(NS_STEPS):
            mix = quintic_a * eye + quintic_b * gram + quintic_c * exact(gram, gram)
            product = mix if step == 0 else exact(product, mix)
            if step < NS_STEPS - 1:
                gram = exact(exact(mix, gram), mix)
        ortho = exact(grad * norm, product)
        osend[...] = ortho.reshape(NZ, 8, HD)
        for index, owner in enumerate(OWNERS):
            @pl.when(z == owner)
            def _(index=index):
                def send_rows(step, carry):
                    there = lax.rem(z + step, NZ)
                    remote(
                        osend.at[there], orecv.at[index], o_send, o_recv.at[index],
                        {"ctx": ctx_id(there, x, k)},
                    ).start()
                    return carry

                lax.fori_loop(1, NZ, send_rows, 0)
                orecv[index] = osend[z]

    bytes_of(halo, halo_recv)
    bytes_of(squares.at[pl.ds(0, 7)], sq_recv)
    spread = squares[0]
    for j in range(1, 8):
        spread = spread + squares[j]
    spread = exact(spread, jnp.full((8, HD), 0.125, F32), ((0,), (0,)))
    scale = lax.rsqrt(spread * (1.0 / (8 * 3 * HD)) + epsilon)
    column = lax.broadcasted_iota(jnp.int32, (PAD, PAD), 1)
    inside = column < FRAME
    inside_back = jnp.logical_and(inside, c > 0)
    inv_sqrt = HD ** (-0.5)
    for h in range(3):
        lanes = slice(h * HD, h * HD + HD)
        query_h = padded(q_ref[:, lanes])
        own = dot(query_h, kv[0, h], ((1,), (1,))) * inv_sqrt
        back = dot(query_h, halo[0, h], ((1,), (1,))) * inv_sqrt
        own = jnp.where(inside, own, -1e30)
        back = jnp.where(inside_back, back, -1e30)
        top = jnp.maximum(jnp.max(own, axis=1, keepdims=True), jnp.max(back, axis=1, keepdims=True))
        own, back = jnp.exp(own - top), jnp.exp(back - top)
        total = jnp.sum(own, axis=1, keepdims=True) + jnp.sum(back, axis=1, keepdims=True)
        attended = dot((own / total).astype(BF), kv[1, h], ((1,), (0,)))
        attended = attended + dot((back / total).astype(BF), halo[1, h], ((1,), (0,)))
        out = attended + fast[h] * gain_ref[0:1, lanes] * scale
        bo_ref[:, lanes] = out[:FRAME].astype(BF)

    for index, owner in enumerate(OWNERS):
        @pl.when(z != owner)
        def _(index=index):
            bytes_of(orecv.at[index], o_recv.at[index])

    for index in range(9):
        weights = fw_ref[index % 3, index // 3]
        summed = weights + orecv[index]
        old = jnp.sqrt(jnp.sum(weights * weights, axis=1, keepdims=True))
        new = lax.rsqrt(jnp.sum(summed * summed, axis=1, keepdims=True) + epsilon)
        nw_ref[index % 3, index // 3] = summed * old * new

    for g in range(3):
        bytes_of(groups[g].at[pl.ds(0, 15)], ag_send.at[g])
        bytes_of(kt.at[g, pl.ds(0, 3)], kt_send.at[g])
        bytes_of(wfull.at[g, pl.ds(0, 3)], wf_send.at[g])
    for index, owner in enumerate(OWNERS):
        @pl.when(z != owner)
        def _(index=index):
            bytes_of(gbuf.at[index], g_send.at[index])

    bytes_of(kv, halo_send)
    bytes_of(squares.at[pl.ds(0, 7)], sq_send)

    @pl.when(is_owner)
    def _():
        bytes_of(osend.at[pl.ds(0, 15)], o_send)


def on_device(queries, keys, values, rates, frame_update, fast_weights, gain):
    vmem = pl.BlockSpec(memory_space=pltpu.VMEM)
    smem = pl.BlockSpec(memory_space=pltpu.SMEM)
    dma = pltpu.SemaphoreType.DMA
    return pl.pallas_call(
        kernel,
        out_shape=(
            jax.ShapeDtypeStruct(queries.shape, BF),
            jax.ShapeDtypeStruct(fast_weights.shape, F32),
        ),
        in_specs=[vmem, vmem, vmem, vmem, smem, vmem, vmem],
        out_specs=(vmem, vmem),
        scratch_shapes=[
            pltpu.VMEM((NZ, 32, HD), BF),
            pltpu.VMEM((NZ, 16, HD), BF),
            pltpu.VMEM((NZ, 32, HD), BF),
            pltpu.VMEM((3, 4, 2, PAD, HD), BF),
            pltpu.VMEM((3, 4, 3 * HD, HD), BF),
            pltpu.VMEM((9, HD, HD), BF),
            pltpu.VMEM((NZ, HD, HD), BF),
            pltpu.VMEM((2, 3, PAD, HD), BF),
            pltpu.VMEM((2, 3, PAD, HD), BF),
            pltpu.VMEM((8, 8, PAD), F32),
            pltpu.VMEM((4, HD, HD), F32),
            pltpu.VMEM((NZ, 8, HD), F32),
            pltpu.VMEM((9, 8, HD), F32),
            dma((3,)), dma((3,)), dma((3,)), dma((3,)), dma((3,)), dma((3,)),
            dma((9,)), dma, dma, dma, dma, dma,
            dma((2,)), dma((2,)), dma, dma((9,)),
        ],
        compiler_params=pltpu.CompilerParams(
            collective_id=0, has_side_effects=True, vmem_limit_bytes=48 * 1024 * 1024
        ),
        name="block",
    )(queries, keys, values, rates, frame_update, fast_weights, gain.reshape(1, -1))


def solution(mesh):
    placed = (
        P("ctx", "head"),
        P("ctx", "head"),
        P("ctx", "head"),
        P("ctx", "head"),
        P("ctx"),
        P(None, "head", "ctx", None),
        P("head"),
    )
    return jax.shard_map(
        on_device,
        mesh=mesh,
        in_specs=placed,
        out_specs=(P("ctx", "head"), P(None, "head", "ctx", None)),
        check_vma=False,
    )
```

```python
import jax
import jax.numpy as jnp
from jax import lax
from jax.experimental import pallas as pl
from jax.experimental.pallas import tpu as pltpu
from jax.sharding import PartitionSpec as P

HD = 128
FRAME = 195
PAD = 208
NS_STEPS = 5
NZ = 16
OWNERS = (0, 5, 11, 2, 7, 12, 4, 9, 14)
MESH = pl.DeviceIdType.MESH
BF = jnp.bfloat16
F32 = jnp.float32

epsilon = 1e-06
quintic_a = 3.4445
quintic_b = -4.775
quintic_c = 2.0315


def dot(a, b, dims, precision=None):
    return lax.dot_general(a, b, (dims, ((), ())), precision=precision, preferred_element_type=F32)


def exact(a, b, dims=((1,), (0,))):
    return dot(a, b, dims, lax.Precision.HIGHEST)


def ctx_id(z, x, k):
    return (z * 2 + x) * 2 + k


def padded(value):
    return jnp.concatenate([value, jnp.zeros((PAD - FRAME, value.shape[1]), value.dtype)], axis=0)


def kernel(
    q_hbm, k_hbm, v_hbm, r_hbm, fu_hbm, fw_hbm, gain_hbm,
    bo_ref, nw_ref,
    q_ref, k_ref, v_ref, r_ref, fu_ref, fw_ref, gain_ref,
    wag_a, wag_b, wag_c, kt, wfull, gbuf, grecv, kv, halo, squares, grams, osend, orecv,
    in_sem, ag_send, ag_recv, relay_recv, kt_send, kt_recv, ktx_recv, wf_send, wf_recv, wfx_recv, g_send, g_recv,
    halo_send, halo_recv, sq_send, sq_recv, gram_send, gram_recv, o_send, o_recv,
):
    c = lax.axis_index("ctx")
    hd = lax.axis_index("head")
    z, x, k = c // 4, lax.rem(c // 2, 2), lax.rem(c, 2)
    quarter = lax.rem(c, 4)
    sibling, across = ctx_id(z, x, 1 - k), ctx_id(z, 1 - x, k)
    across_quarter = (1 - x) * 2 + k
    peers = [sibling, across, ctx_id(z, 1 - x, 1 - k)]
    loads = [
        pltpu.make_async_copy(src, dst, in_sem.at[i])
        for i, (src, dst) in enumerate(
            (
                (fw_hbm, fw_ref), (k_hbm, k_ref), (v_hbm, v_ref), (r_hbm, r_ref),
                (fu_hbm, fu_ref), (q_hbm, q_ref), (gain_hbm, gain_ref),
            )
        )
    ]
    for load in loads:
        load.start()
    after, before = lax.rem(c + 1, 64), lax.rem(c + 63, 64)

    barrier = pltpu.get_barrier_semaphore()

    def greet_line(step, carry):
        there = ctx_id(lax.rem(z + step, NZ), x, k)
        pl.semaphore_signal(barrier, inc=1, device_id={"ctx": there}, device_id_type=MESH)
        return carry

    def greet_head(step, carry):
        pl.semaphore_signal(
            barrier, inc=1, device_id={"head": lax.rem(hd + step, 8)}, device_id_type=MESH
        )
        return carry

    lax.fori_loop(1, NZ, greet_line, 0)
    lax.fori_loop(1, 8, greet_head, 0)
    for peer in peers:
        pl.semaphore_signal(barrier, inc=1, device_id={"ctx": peer}, device_id_type=MESH)
    last, first = quarter == 3, quarter == 0

    @pl.when(last)
    def _():
        pl.semaphore_signal(barrier, inc=1, device_id={"ctx": after}, device_id_type=MESH)

    @pl.when(first)
    def _():
        pl.semaphore_signal(barrier, inc=1, device_id={"ctx": before}, device_id_type=MESH)

    loads[0].wait()

    def block(index):
        return fw_ref[index % 3, index // 3]

    def pair(index):
        second = block(index + 1) if index < 8 else jnp.zeros((8, HD), F32)
        return jnp.concatenate([block(index), second], axis=0).astype(BF)

    wag_a[z, 0:16] = pair(0)
    wag_a[z, 16:32] = pair(2)
    wag_b[z] = pair(4)
    wag_c[z, 0:16] = pair(6)
    wag_c[z, 16:32] = pair(8)
    groups = (wag_a, wag_b, wag_c)

    for load in loads[1:]:
        load.wait()
    keep = fu_ref[0].astype(F32)
    rates = r_ref[...] * keep
    heads_row = lax.broadcasted_iota(jnp.int32, (3, HD), 0)
    for h in range(3):
        lanes = slice(h * HD, h * HD + HD)
        key_h, value_h = k_ref[:, lanes], v_ref[:, lanes]
        rate = exact(rates, (heads_row == h).astype(F32), ((0,), (0,)))
        target = (rate * value_h.astype(F32)).astype(BF)
        key_h = padded(key_h)
        kt[h, quarter, 0] = key_h
        kt[h, quarter, 1] = padded(target)
        kv[0, h] = key_h
        kv[1, h] = padded(value_h)

    pl.semaphore_wait(barrier, 25 + last.astype(jnp.int32) + first.astype(jnp.int32))

    def remote(src, dst, send, recv, device):
        return pltpu.make_async_remote_copy(
            src_ref=src, dst_ref=dst, send_sem=send, recv_sem=recv, device_id=device, device_id_type=MESH
        )

    def bytes_of(ref, sem):
        pltpu.make_async_copy(ref, ref, sem).wait()

    def line(step):
        return {"ctx": ctx_id(lax.rem(z + step + NZ, NZ), x, k)}

    def shard(g, source, step, recv):
        there = groups[g].at[source]
        remote(there, there, ag_send.at[g], recv, line(step)).start()

    for g in range(3):
        for i, step in enumerate((3, -3, 6, -6)):
            shard(g, z, step, relay_recv.at[g, i])
        for step in (1, -1):
            shard(g, z, step, ag_recv.at[g])
        mine = kt.at[g, quarter]
        remote(mine, mine, kt_send.at[g], ktx_recv.at[g], {"ctx": across}).start()
        remote(mine, mine, kt_send.at[g], kt_recv.at[g], {"ctx": sibling}).start()

    def hand_on(g, i):
        step = (3, -3, 6, -6)[i]
        source = lax.rem(z - step + NZ, NZ)
        bytes_of(groups[g].at[source], relay_recv.at[g, i])
        for beside in (1, -1):
            shard(g, source, beside, ag_recv.at[g])
        if i >= 2:
            @pl.when(k == i - 2)
            def _():
                shard(g, source, step // 3, ag_recv.at[g])

    def hand_keys(h):
        other = kt.at[h, across_quarter]
        bytes_of(other, ktx_recv.at[h])
        remote(other, other, kt_send.at[h], kt_recv.at[h], {"ctx": sibling}).start()

    for i in (0, 1):
        for g in range(3):
            hand_on(g, i)
    hand_keys(0)
    for g in range(3):
        hand_on(g, 2)
        hand_on(g, 3)
    hand_keys(1)
    hand_keys(2)

    def weight_block(index):
        group, tile = ((0, 0), (0, 1), (1, 0), (2, 0), (2, 1))[index // 2]
        both = groups[group][:, tile * 16 : tile * 16 + 16, :].astype(F32)
        half = both.reshape(NZ, 2, 8, HD)[:, index % 2]
        return half.reshape(HD, HD).astype(BF)

    for h in range(3):
        if h == 0:
            bytes_of(wag_a.at[pl.ds(0, 11)], ag_recv.at[0])
        elif h == 1:
            bytes_of(wag_b.at[pl.ds(0, 11)], ag_recv.at[1])
        else:
            bytes_of(wag_c.at[pl.ds(0, 11)], ag_recv.at[2])
        for m in range(3):
            wfull[h, quarter, m * HD : m * HD + HD] = weight_block(h * 3 + m)
        mine = wfull.at[h, quarter]
        remote(mine, mine, wf_send.at[h], wfx_recv.at[h], {"ctx": across}).start()
        remote(mine, mine, wf_send.at[h], wf_recv.at[h], {"ctx": sibling}).start()
        bytes_of(kt.at[h, pl.ds(0, 2)], kt_recv.at[h])
        w13 = wfull[h, quarter, 0 : 2 * HD]
        w2 = wfull[h, quarter, 2 * HD : 3 * HD]
        grad13 = jnp.zeros((2 * HD, HD), F32)
        grad2 = jnp.zeros((HD, HD), F32)
        for j in range(4):
            key_j, target_j = kt[h, j, 0], kt[h, j, 1]
            pre = dot(key_j, w13, ((1,), (1,)))
            pre_one, pre_three = pre[:, :HD], pre[:, HD:]
            back = dot(target_j, w2, ((1,), (1,)))
            sig = jax.nn.sigmoid(pre_one)
            gate = pre_one * sig
            act = (gate * pre_three).astype(BF)
            delta_one = (back * pre_three * sig * (1.0 + pre_one * (1.0 - sig))).astype(BF)
            delta_three = (back * gate).astype(BF)
            delta = jnp.concatenate([delta_one, delta_three], axis=1)
            grad13 = grad13 + dot(delta, key_j, ((0,), (0,)))
            grad2 = grad2 + dot(act, target_j, ((0,), (0,)))
        for m, grad in enumerate((grad13[:HD], grad13[HD:], grad2)):
            index = h * 3 + m
            owner = OWNERS[index]
            gbuf[index] = grad.astype(BF)

            @pl.when(z != owner)
            def _(index=index, owner=owner):
                remote(
                    gbuf.at[index], grecv.at[z], g_send.at[index], g_recv, {"ctx": ctx_id(owner, x, k)}
                ).start()

            @pl.when(z == owner)
            def _(grad=grad):
                grecv[z] = grad.astype(BF)

    remote(kv, halo, halo_send, halo_recv, {"ctx": after}).start()

    fast = []
    for h in range(3):
        other = wfull.at[h, across_quarter]
        bytes_of(other, wfx_recv.at[h])
        remote(other, other, wf_send.at[h], wf_recv.at[h], {"ctx": sibling}).start()
    for h in range(3):
        bytes_of(wfull.at[h, pl.ds(0, 2)], wf_recv.at[h])
        query_h = padded(q_ref[:, h * HD : h * HD + HD])
        total = jnp.zeros((PAD, HD), F32)
        for j in range(4):
            proj = dot(query_h, wfull[h, j, 0 : 2 * HD], ((1,), (1,)))
            one, three = proj[:, :HD], proj[:, HD:]
            hidden = (one * jax.nn.sigmoid(one) * three).astype(BF)
            total = total + dot(hidden, wfull[h, j, 2 * HD : 3 * HD], ((1,), (0,)))
        fast.append(total)
    square_sum = fast[0] * fast[0] + fast[1] * fast[1] + fast[2] * fast[2]
    squares[hd] = exact(jnp.ones((8, HD), F32), square_sum, ((1,), (1,)))

    def send_squares(step, carry):
        there = lax.rem(hd + step, 8)
        remote(squares.at[hd], squares.at[hd], sq_send, sq_recv, {"head": there}).start()
        return carry

    lax.fori_loop(1, 8, send_squares, 0)

    is_owner = z == OWNERS[0]
    for owner in OWNERS[1:]:
        is_owner = jnp.logical_or(is_owner, z == owner)

    @pl.when(is_owner)
    def _():
        bytes_of(grecv.at[pl.ds(0, 15)], g_recv)
        grad = grecv[0].astype(F32)
        for j in range(1, NZ):
            grad = grad + grecv[j].astype(F32)
        grams[0] = exact(grad, grad, ((0,), (0,)))
        copy = remote(grams.at[0], grams.at[1], gram_send.at[0], gram_recv.at[0], {"ctx": peers[0]})
        copy.start()
        copy.wait()
        grams[2] = grams[0] + grams[1]
        copy = remote(grams.at[2], grams.at[3], gram_send.at[1], gram_recv.at[1], {"ctx": peers[1]})
        copy.start()
        copy.wait()
        gram = grams[2] + grams[3]
        rows = lax.broadcasted_iota(jnp.int32, (HD, HD), 0)
        columns = lax.broadcasted_iota(jnp.int32, (HD, HD), 1)
        eye = (rows == columns).astype(F32)
        norm = lax.rsqrt(jnp.sum(jnp.sum(gram * eye, axis=0, keepdims=True), axis=1, keepdims=True) + epsilon)
        gram = gram * (norm * norm)
        product = None
        for step in range(NS_STEPS):
            mix = quintic_a * eye + quintic_b * gram + quintic_c * exact(gram, gram)
            product = mix if step == 0 else exact(product, mix)
            if step < NS_STEPS - 1:
                gram = exact(exact(mix, gram), mix)
        ortho = exact(grad * norm, product)
        osend[...] = ortho.reshape(NZ, 8, HD)
        for index, owner in enumerate(OWNERS):
            @pl.when(z == owner)
            def _(index=index):
                def send_rows(step, carry):
                    there = lax.rem(z + step, NZ)
                    remote(
                        osend.at[there], orecv.at[index], o_send, o_recv.at[index],
                        {"ctx": ctx_id(there, x, k)},
                    ).start()
                    return carry

                lax.fori_loop(1, NZ, send_rows, 0)
                orecv[index] = osend[z]

    bytes_of(halo, halo_recv)
    bytes_of(squares.at[pl.ds(0, 7)], sq_recv)
    spread = squares[0]
    for j in range(1, 8):
        spread = spread + squares[j]
    spread = exact(spread, jnp.full((8, HD), 0.125, F32), ((0,), (0,)))
    scale = lax.rsqrt(spread * (1.0 / (8 * 3 * HD)) + epsilon)
    column = lax.broadcasted_iota(jnp.int32, (PAD, PAD), 1)
    inside = column < FRAME
    inside_back = jnp.logical_and(inside, c > 0)
    inv_sqrt = HD ** (-0.5)
    for h in range(3):
        lanes = slice(h * HD, h * HD + HD)
        query_h = padded(q_ref[:, lanes])
        own = dot(query_h, kv[0, h], ((1,), (1,))) * inv_sqrt
        back = dot(query_h, halo[0, h], ((1,), (1,))) * inv_sqrt
        own = jnp.where(inside, own, -1e30)
        back = jnp.where(inside_back, back, -1e30)
        top = jnp.maximum(jnp.max(own, axis=1, keepdims=True), jnp.max(back, axis=1, keepdims=True))
        own, back = jnp.exp(own - top), jnp.exp(back - top)
        total = jnp.sum(own, axis=1, keepdims=True) + jnp.sum(back, axis=1, keepdims=True)
        attended = dot((own / total).astype(BF), kv[1, h], ((1,), (0,)))
        attended = attended + dot((back / total).astype(BF), halo[1, h], ((1,), (0,)))
        out = attended + fast[h] * gain_ref[lanes][None, :] * scale
        bo_ref[:, lanes] = out[:FRAME].astype(BF)

    for index, owner in enumerate(OWNERS):
        @pl.when(z != owner)
        def _(index=index):
            bytes_of(orecv.at[index], o_recv.at[index])

    for index in range(9):
        weights = fw_ref[index % 3, index // 3]
        summed = weights + orecv[index]
        old = jnp.sqrt(jnp.sum(weights * weights, axis=1, keepdims=True))
        new = lax.rsqrt(jnp.sum(summed * summed, axis=1, keepdims=True) + epsilon)
        nw_ref[index % 3, index // 3] = summed * old * new

    for g in range(3):
        bytes_of(groups[g].at[pl.ds(0, 15)], ag_send.at[g])
        bytes_of(kt.at[g, pl.ds(0, 3)], kt_send.at[g])
        bytes_of(wfull.at[g, pl.ds(0, 3)], wf_send.at[g])
    for index, owner in enumerate(OWNERS):
        @pl.when(z != owner)
        def _(index=index):
            bytes_of(gbuf.at[index], g_send.at[index])

    bytes_of(kv, halo_send)
    bytes_of(squares.at[pl.ds(0, 7)], sq_send)

    @pl.when(is_owner)
    def _():
        bytes_of(osend.at[pl.ds(0, 15)], o_send)


def on_device(queries, keys, values, rates, frame_update, fast_weights, gain):
    arrays = (queries, keys, values, rates.T, frame_update, fast_weights, gain)
    vmem = pl.BlockSpec(memory_space=pltpu.VMEM)
    hbm = pl.BlockSpec(memory_space=pltpu.HBM)
    dma = pltpu.SemaphoreType.DMA
    return pl.pallas_call(
        kernel,
        out_shape=(
            jax.ShapeDtypeStruct(queries.shape, BF),
            jax.ShapeDtypeStruct(fast_weights.shape, F32),
        ),
        in_specs=[hbm] * 7,
        out_specs=(vmem, vmem),
        scratch_shapes=[
            pltpu.VMEM(queries.shape, BF),
            pltpu.VMEM(keys.shape, BF),
            pltpu.VMEM(values.shape, BF),
            pltpu.VMEM((3, FRAME), F32),
            pltpu.SMEM(frame_update.shape, jnp.int32),
            pltpu.VMEM(fast_weights.shape, F32),
            pltpu.VMEM(gain.shape, F32),
            pltpu.VMEM((NZ, 32, HD), BF),
            pltpu.VMEM((NZ, 16, HD), BF),
            pltpu.VMEM((NZ, 32, HD), BF),
            pltpu.VMEM((3, 4, 2, PAD, HD), BF),
            pltpu.VMEM((3, 4, 3 * HD, HD), BF),
            pltpu.VMEM((9, HD, HD), BF),
            pltpu.VMEM((NZ, HD, HD), BF),
            pltpu.VMEM((2, 3, PAD, HD), BF),
            pltpu.VMEM((2, 3, PAD, HD), BF),
            pltpu.VMEM((8, 8, PAD), F32),
            pltpu.VMEM((4, HD, HD), F32),
            pltpu.VMEM((NZ, 8, HD), F32),
            pltpu.VMEM((9, 8, HD), F32),
            dma((7,)), dma((3,)), dma((3,)), dma((3, 4)), dma((3,)), dma((3,)), dma((3,)), dma((3,)), dma((3,)), dma((3,)),
            dma((9,)), dma, dma, dma, dma, dma,
            dma((2,)), dma((2,)), dma, dma((9,)),
        ],
        compiler_params=pltpu.CompilerParams(
            collective_id=0, has_side_effects=True, vmem_limit_bytes=48 * 1024 * 1024
        ),
        name="block",
    )(*[
        array if array.size == 1 else pltpu.with_memory_space_constraint(array, pltpu.HBM)
        for array in arrays
    ])


def solution(mesh):
    placed = (
        P("ctx", "head"),
        P("ctx", "head"),
        P("ctx", "head"),
        P("ctx", "head"),
        P("ctx"),
        P(None, "head", "ctx", None),
        P("head"),
    )
    return jax.shard_map(
        on_device,
        mesh=mesh,
        in_specs=placed,
        out_specs=(P("ctx", "head"), P(None, "head", "ctx", None)),
        check_vma=False,
    )
```

```python
import jax
import jax.numpy as jnp
from jax import lax
from jax.experimental import pallas as pl
from jax.experimental.pallas import tpu as pltpu
from jax.sharding import PartitionSpec as P

HD = 128
FRAME = 195
PAD = 208
NS_STEPS = 5
NZ = 16
OWNERS = (5, 9, 11, 2, 7, 12, 0, 4, 14)
RELAYED = (True, True, True)
TOPS = (0, 1, 15, 3, 13, 6, 10)
MESH = pl.DeviceIdType.MESH
BF = jnp.bfloat16
F32 = jnp.float32

epsilon = 1e-06
quintic_a = 3.4445
quintic_b = -4.775
quintic_c = 2.0315


def dot(a, b, dims, precision=None):
    return lax.dot_general(a, b, (dims, ((), ())), precision=precision, preferred_element_type=F32)


def exact(a, b, dims=((1,), (0,))):
    return dot(a, b, dims, lax.Precision.HIGHEST)


def ctx_id(z, x, k):
    return (z * 2 + x) * 2 + k


def padded(value):
    return jnp.concatenate([value, jnp.zeros((PAD - FRAME, value.shape[1]), value.dtype)], axis=0)


def kernel(
    q_hbm, k_hbm, v_hbm, r_hbm, fu_hbm, fw_hbm, gain_hbm,
    bo_ref, nw_ref,
    q_ref, k_ref, v_ref, r_ref, fu_ref, fw_ref, gain_ref,
    wag_a, wag_b, wag_c, kt, wfull, gbuf, rbuf, grecv, gsum, kv, halo, squares, grams, osend, orecv,
    in_sem, ag_send, ag_recv, relay_recv, kt_send, kt_recv, ktx_recv, wf_send, wf_recv, wfx_recv, g_send, r_recv, g_recv,
    halo_send, halo_recv, sq_send, sq_recv, gram_send, gram_recv, o_send, o_recv,
):
    c = lax.axis_index("ctx")
    hd = lax.axis_index("head")
    z, x, k = c // 4, lax.rem(c // 2, 2), lax.rem(c, 2)
    quarter = lax.rem(c, 4)
    sibling, across = ctx_id(z, x, 1 - k), ctx_id(z, 1 - x, k)
    across_quarter = (1 - x) * 2 + k
    peers = [sibling, across, ctx_id(z, 1 - x, 1 - k)]
    loads = [
        pltpu.make_async_copy(src, dst, in_sem.at[i])
        for i, (src, dst) in enumerate(
            (
                (fw_hbm, fw_ref), (k_hbm, k_ref), (v_hbm, v_ref), (r_hbm, r_ref),
                (fu_hbm, fu_ref), (q_hbm, q_ref), (gain_hbm, gain_ref),
            )
        )
    ]
    for load in loads:
        load.start()
    after, before = lax.rem(c + 1, 64), lax.rem(c + 63, 64)

    barrier = pltpu.get_barrier_semaphore()

    def greet_head(step, carry):
        pl.semaphore_signal(
            barrier, inc=1, device_id={"head": lax.rem(hd + step, 8)}, device_id_type=MESH
        )
        return carry

    for step in (1, 2, 3, 6, 10, 13, 14, 15):
        there = ctx_id(lax.rem(z + step, NZ), x, k)
        pl.semaphore_signal(barrier, inc=1, device_id={"ctx": there}, device_id_type=MESH)
    lax.fori_loop(1, 8, greet_head, 0)
    for peer in peers:
        pl.semaphore_signal(barrier, inc=1, device_id={"ctx": peer}, device_id_type=MESH)
    last, first = quarter == 3, quarter == 0

    @pl.when(last)
    def _():
        pl.semaphore_signal(barrier, inc=1, device_id={"ctx": after}, device_id_type=MESH)

    @pl.when(first)
    def _():
        pl.semaphore_signal(barrier, inc=1, device_id={"ctx": before}, device_id_type=MESH)

    loads[0].wait()

    def block(index):
        return fw_ref[index % 3, index // 3]

    def pair(index):
        second = block(index + 1) if index < 8 else jnp.zeros((8, HD), F32)
        return jnp.concatenate([block(index), second], axis=0).astype(BF)

    wag_a[z, 0:16] = pair(0)
    wag_a[z, 16:32] = pair(2)
    wag_b[z] = pair(4)
    wag_c[z, 0:16] = pair(6)
    wag_c[z, 16:32] = pair(8)
    groups = (wag_a, wag_b, wag_c)

    for load in loads[1:]:
        load.wait()
    keep = fu_ref[0].astype(F32)
    rates = r_ref[...] * keep
    heads_row = lax.broadcasted_iota(jnp.int32, (3, HD), 0)
    for h in range(3):
        lanes = slice(h * HD, h * HD + HD)
        key_h, value_h = k_ref[:, lanes], v_ref[:, lanes]
        rate = exact(rates, (heads_row == h).astype(F32), ((0,), (0,)))
        target = (rate * value_h.astype(F32)).astype(BF)
        key_h = padded(key_h)
        kt[h, quarter, 0] = key_h
        kt[h, quarter, 1] = padded(target)
        kv[0, h] = key_h
        kv[1, h] = padded(value_h)

    pl.semaphore_wait(barrier, 18 + last.astype(jnp.int32) + first.astype(jnp.int32))

    def remote(src, dst, send, recv, device):
        return pltpu.make_async_remote_copy(
            src_ref=src, dst_ref=dst, send_sem=send, recv_sem=recv, device_id=device, device_id_type=MESH
        )

    def bytes_of(ref, sem):
        pltpu.make_async_copy(ref, ref, sem).wait()

    def line(step):
        return {"ctx": ctx_id(lax.rem(z + step + NZ, NZ), x, k)}

    def shard(g, source, step, recv):
        there = groups[g].at[source]
        remote(there, there, ag_send.at[g], recv, line(step)).start()

    for g in range(3):
        for i, step in enumerate((3, -3, 6, -6)):
            shard(g, z, step, relay_recv.at[g, i])
        for step in (1, -1):
            shard(g, z, step, ag_recv.at[g])
        mine = kt.at[g, quarter]
        remote(mine, mine, kt_send.at[g], ktx_recv.at[g], {"ctx": across}).start()
        remote(mine, mine, kt_send.at[g], kt_recv.at[g], {"ctx": sibling}).start()

    def hand_on(g, i):
        step = (3, -3, 6, -6)[i]
        source = lax.rem(z - step + NZ, NZ)
        bytes_of(groups[g].at[source], relay_recv.at[g, i])
        for beside in (1, -1):
            shard(g, source, beside, ag_recv.at[g])
        if i >= 2:
            @pl.when(k == i - 2)
            def _():
                shard(g, source, step // 3, ag_recv.at[g])

    def hand_keys(h):
        other = kt.at[h, across_quarter]
        bytes_of(other, ktx_recv.at[h])
        remote(other, other, kt_send.at[h], kt_recv.at[h], {"ctx": sibling}).start()

    for i in (0, 1):
        for g in range(3):
            hand_on(g, i)
    hand_keys(0)
    for g in range(3):
        hand_on(g, 2)
        hand_on(g, 3)
    hand_keys(1)
    hand_keys(2)

    def weight_block(index):
        group, tile = ((0, 0), (0, 1), (1, 0), (2, 0), (2, 1))[index // 2]
        both = groups[group][:, tile * 16 : tile * 16 + 16, :].astype(F32)
        half = both.reshape(NZ, 2, 8, HD)[:, index % 2]
        return half.reshape(HD, HD).astype(BF)

    def is_sum(index):
        return jnp.logical_and(z == OWNERS[index], k == index % 2)

    def to_sum(index):
        return {"ctx": ctx_id(OWNERS[index], x, index % 2)}

    def is_leaf(away):
        leaf = away == 8
        for step in (2, 4, 5, 7, 9, 11, 12, 14):
            leaf = jnp.logical_or(leaf, away == step)
        return leaf

    def relay_head(h):
        if not RELAYED[h]:
            return
        for index in range(h * 3, h * 3 + 3):
            away = lax.rem(z - OWNERS[index] + NZ, NZ)
            six = jnp.logical_or(away == 6, away == 10)
            three = jnp.logical_or(away == 3, away == 13)
            extra = jnp.logical_or(
                jnp.logical_and(away == 6, k == 0), jnp.logical_and(away == 10, k == 1)
            )

            @pl.when(jnp.logical_or(six, three))
            def _(index=index, extra=extra):
                bytes_of(rbuf.at[index, pl.ds(0, 2)], r_recv.at[index, 0])
                gbuf[index] = (
                    gbuf[index].astype(F32) + rbuf[index, 0].astype(F32) + rbuf[index, 1].astype(F32)
                ).astype(BF)

            @pl.when(extra)
            def _(index=index):
                bytes_of(rbuf.at[index, 2], r_recv.at[index, 1])
                gbuf[index] = (gbuf[index].astype(F32) + rbuf[index, 2].astype(F32)).astype(BF)

            place = sum((jnp.where(away == top, t, 0) for t, top in enumerate(TOPS)), 0)
            slot = k * len(TOPS) + place

            @pl.when(jnp.logical_not(jnp.logical_or(is_leaf(away), is_sum(index))))
            def _(index=index, slot=slot):
                remote(gbuf.at[index], grecv.at[slot], g_send.at[index], g_recv, to_sum(index)).start()

            @pl.when(is_sum(index))
            def _(index=index, slot=slot):
                grecv[slot] = gbuf[index]

    for h in range(3):
        if h == 0:
            bytes_of(wag_a.at[pl.ds(0, 11)], ag_recv.at[0])
        elif h == 1:
            bytes_of(wag_b.at[pl.ds(0, 11)], ag_recv.at[1])
        else:
            bytes_of(wag_c.at[pl.ds(0, 11)], ag_recv.at[2])
        for m in range(3):
            wfull[h, quarter, m * HD : m * HD + HD] = weight_block(h * 3 + m)
        mine = wfull.at[h, quarter]
        remote(mine, mine, wf_send.at[h], wfx_recv.at[h], {"ctx": across}).start()
        remote(mine, mine, wf_send.at[h], wf_recv.at[h], {"ctx": sibling}).start()
        bytes_of(kt.at[h, pl.ds(0, 2)], kt_recv.at[h])
        w13 = wfull[h, quarter, 0 : 2 * HD]
        w2 = wfull[h, quarter, 2 * HD : 3 * HD]
        grad13 = jnp.zeros((2 * HD, HD), F32)
        grad2 = jnp.zeros((HD, HD), F32)
        for j in range(4):
            key_j, target_j = kt[h, j, 0], kt[h, j, 1]
            pre = dot(key_j, w13, ((1,), (1,)))
            pre_one, pre_three = pre[:, :HD], pre[:, HD:]
            back = dot(target_j, w2, ((1,), (1,)))
            sig = jax.nn.sigmoid(pre_one)
            gate = pre_one * sig
            act = (gate * pre_three).astype(BF)
            delta_one = (back * pre_three * sig * (1.0 + pre_one * (1.0 - sig))).astype(BF)
            delta_three = (back * gate).astype(BF)
            delta = jnp.concatenate([delta_one, delta_three], axis=1)
            grad13 = grad13 + dot(delta, key_j, ((0,), (0,)))
            grad2 = grad2 + dot(act, target_j, ((0,), (0,)))
        for m, grad in enumerate((grad13[:HD], grad13[HD:], grad2)):
            index = h * 3 + m
            owner = OWNERS[index]
            gbuf[index] = grad.astype(BF)

            if not RELAYED[h]:
                slot = k * NZ + z

                @pl.when(jnp.logical_not(is_sum(index)))
                def _(index=index, slot=slot):
                    remote(gbuf.at[index], grecv.at[slot], g_send.at[index], g_recv, to_sum(index)).start()

                @pl.when(is_sum(index))
                def _(index=index, slot=slot):
                    grecv[slot] = gbuf[index]
            else:
                away = lax.rem(z - owner + NZ, NZ)
                relay = jnp.where(
                    away == 8, jnp.where(k == 0, 6, 10),
                    jnp.where(away < 8, jnp.where(away < 5, 3, 6), jnp.where(away > 11, 13, 10)),
                )
                slot = jnp.where(away == 8, 2, jnp.where(away < relay, 0, 1))
                leaf = is_leaf(away)

                @pl.when(leaf)
                def _(index=index, owner=owner, relay=relay, slot=slot):
                    remote(
                        gbuf.at[index], rbuf.at[index, slot], g_send.at[index], r_recv.at[index, slot // 2],
                        {"ctx": ctx_id(lax.rem(relay + owner, NZ), x, k)},
                    ).start()
        if h > 0:
            relay_head(h - 1)
    relay_head(2)

    remote(kv, halo, halo_send, halo_recv, {"ctx": after}).start()

    fast = []
    for h in range(3):
        other = wfull.at[h, across_quarter]
        bytes_of(other, wfx_recv.at[h])
        remote(other, other, wf_send.at[h], wf_recv.at[h], {"ctx": sibling}).start()
    for h in range(3):
        bytes_of(wfull.at[h, pl.ds(0, 2)], wf_recv.at[h])
        query_h = padded(q_ref[:, h * HD : h * HD + HD])
        total = jnp.zeros((PAD, HD), F32)
        for j in range(4):
            proj = dot(query_h, wfull[h, j, 0 : 2 * HD], ((1,), (1,)))
            one, three = proj[:, :HD], proj[:, HD:]
            hidden = (one * jax.nn.sigmoid(one) * three).astype(BF)
            total = total + dot(hidden, wfull[h, j, 2 * HD : 3 * HD], ((1,), (0,)))
        fast.append(total)
    square_sum = fast[0] * fast[0] + fast[1] * fast[1] + fast[2] * fast[2]
    squares[hd] = exact(jnp.ones((8, HD), F32), square_sum, ((1,), (1,)))

    def send_squares(step, carry):
        there = lax.rem(hd + step, 8)
        remote(squares.at[hd], squares.at[hd], sq_send, sq_recv, {"head": there}).start()
        return carry

    lax.fori_loop(1, 8, send_squares, 0)

    is_owner = is_sum(0)
    for index in range(1, 9):
        is_owner = jnp.logical_or(is_owner, is_sum(index))

    for index in range(9):
        @pl.when(is_sum(index))
        def _(index=index):
            count = len(TOPS) if RELAYED[index // 3] else NZ
            bytes_of(grecv.at[pl.ds(0, 2 * count - 1)], g_recv)
            for core in range(2):
                total = grecv[core * count].astype(F32)
                for j in range(1, count):
                    total = total + grecv[core * count + j].astype(F32)
                gsum[core * HD : core * HD + HD] = total

    @pl.when(is_owner)
    def _():
        grad = gsum[...]
        grams[0] = exact(grad, grad, ((0,), (0,)))
        copy = remote(grams.at[0], grams.at[1], gram_send, gram_recv, {"ctx": across})
        copy.start()
        copy.wait()
        gram = grams[0] + grams[1]
        rows = lax.broadcasted_iota(jnp.int32, (HD, HD), 0)
        columns = lax.broadcasted_iota(jnp.int32, (HD, HD), 1)
        eye = (rows == columns).astype(F32)
        norm = lax.rsqrt(jnp.sum(jnp.sum(gram * eye, axis=0, keepdims=True), axis=1, keepdims=True) + epsilon)
        gram = gram * (norm * norm)
        product = None
        for step in range(NS_STEPS):
            mix = quintic_a * eye + quintic_b * gram + quintic_c * exact(gram, gram)
            product = mix if step == 0 else exact(product, mix)
            if step < NS_STEPS - 1:
                gram = exact(exact(mix, gram), mix)
        ortho = exact(grad * norm, product)
        osend[...] = ortho.reshape(2, NZ, 8, HD)

    for index in range(9):
        @pl.when(is_sum(index))
        def _(index=index):
            def send_rows(there, carry):
                for core in range(2):
                    @pl.when(jnp.logical_or(there != z, core != k))
                    def _(core=core):
                        remote(
                            osend.at[core, there], orecv.at[index], o_send, o_recv.at[index],
                            {"ctx": ctx_id(there, x, core)},
                        ).start()
                return carry

            lax.fori_loop(0, NZ, send_rows, 0)
            orecv[index] = osend[k, z]

    bytes_of(halo, halo_recv)
    bytes_of(squares.at[pl.ds(0, 7)], sq_recv)
    spread = squares[0]
    for j in range(1, 8):
        spread = spread + squares[j]
    spread = exact(spread, jnp.full((8, HD), 0.125, F32), ((0,), (0,)))
    scale = lax.rsqrt(spread * (1.0 / (8 * 3 * HD)) + epsilon)
    column = lax.broadcasted_iota(jnp.int32, (PAD, PAD), 1)
    inside = column < FRAME
    inside_back = jnp.logical_and(inside, c > 0)
    inv_sqrt = HD ** (-0.5)
    for h in range(3):
        lanes = slice(h * HD, h * HD + HD)
        query_h = padded(q_ref[:, lanes])
        own = dot(query_h, kv[0, h], ((1,), (1,))) * inv_sqrt
        back = dot(query_h, halo[0, h], ((1,), (1,))) * inv_sqrt
        own = jnp.where(inside, own, -1e30)
        back = jnp.where(inside_back, back, -1e30)
        top = jnp.maximum(jnp.max(own, axis=1, keepdims=True), jnp.max(back, axis=1, keepdims=True))
        own, back = jnp.exp(own - top), jnp.exp(back - top)
        total = jnp.sum(own, axis=1, keepdims=True) + jnp.sum(back, axis=1, keepdims=True)
        attended = dot((own / total).astype(BF), kv[1, h], ((1,), (0,)))
        attended = attended + dot((back / total).astype(BF), halo[1, h], ((1,), (0,)))
        out = attended + fast[h] * gain_ref[lanes][None, :] * scale
        bo_ref[:, lanes] = out[:FRAME].astype(BF)

    for index in range(9):
        @pl.when(jnp.logical_not(is_sum(index)))
        def _(index=index):
            bytes_of(orecv.at[index], o_recv.at[index])

    for index in range(9):
        weights = fw_ref[index % 3, index // 3]
        summed = weights + orecv[index]
        old = jnp.sqrt(jnp.sum(weights * weights, axis=1, keepdims=True))
        new = lax.rsqrt(jnp.sum(summed * summed, axis=1, keepdims=True) + epsilon)
        nw_ref[index % 3, index // 3] = summed * old * new

    for g in range(3):
        bytes_of(groups[g].at[pl.ds(0, 15)], ag_send.at[g])
        bytes_of(kt.at[g, pl.ds(0, 3)], kt_send.at[g])
        bytes_of(wfull.at[g, pl.ds(0, 3)], wf_send.at[g])
    for index in range(9):
        @pl.when(jnp.logical_not(is_sum(index)))
        def _(index=index):
            bytes_of(gbuf.at[index], g_send.at[index])

    bytes_of(kv, halo_send)
    bytes_of(squares.at[pl.ds(0, 7)], sq_send)

    @pl.when(is_owner)
    def _():
        bytes_of(osend.at[0], o_send)
        bytes_of(osend.at[1, pl.ds(0, 15)], o_send)


def on_device(queries, keys, values, rates, frame_update, fast_weights, gain):
    arrays = (queries, keys, values, rates.T, frame_update, fast_weights, gain)
    vmem = pl.BlockSpec(memory_space=pltpu.VMEM)
    hbm = pl.BlockSpec(memory_space=pltpu.HBM)
    dma = pltpu.SemaphoreType.DMA
    return pl.pallas_call(
        kernel,
        out_shape=(
            jax.ShapeDtypeStruct(queries.shape, BF),
            jax.ShapeDtypeStruct(fast_weights.shape, F32),
        ),
        in_specs=[hbm] * 7,
        out_specs=(vmem, vmem),
        scratch_shapes=[
            pltpu.VMEM(queries.shape, BF),
            pltpu.VMEM(keys.shape, BF),
            pltpu.VMEM(values.shape, BF),
            pltpu.VMEM((3, FRAME), F32),
            pltpu.SMEM(frame_update.shape, jnp.int32),
            pltpu.VMEM(fast_weights.shape, F32),
            pltpu.VMEM(gain.shape, F32),
            pltpu.VMEM((NZ, 32, HD), BF),
            pltpu.VMEM((NZ, 16, HD), BF),
            pltpu.VMEM((NZ, 32, HD), BF),
            pltpu.VMEM((3, 4, 2, PAD, HD), BF),
            pltpu.VMEM((3, 4, 3 * HD, HD), BF),
            pltpu.VMEM((9, HD, HD), BF),
            pltpu.VMEM((9, 3, HD, HD), BF),
            pltpu.VMEM((2 * NZ, HD, HD), BF),
            pltpu.VMEM((2 * HD, HD), F32),
            pltpu.VMEM((2, 3, PAD, HD), BF),
            pltpu.VMEM((2, 3, PAD, HD), BF),
            pltpu.VMEM((8, 8, PAD), F32),
            pltpu.VMEM((2, HD, HD), F32),
            pltpu.VMEM((2, NZ, 8, HD), F32),
            pltpu.VMEM((9, 8, HD), F32),
            dma((7,)), dma((3,)), dma((3,)), dma((3, 4)), dma((3,)), dma((3,)), dma((3,)), dma((3,)), dma((3,)), dma((3,)),
            dma((9,)), dma((9, 2)), dma, dma, dma, dma, dma,
            dma, dma, dma, dma((9,)),
        ],
        compiler_params=pltpu.CompilerParams(
            collective_id=0, has_side_effects=True, vmem_limit_bytes=48 * 1024 * 1024
        ),
        name="block",
    )(*[
        array if array.size == 1 else pltpu.with_memory_space_constraint(array, pltpu.HBM)
        for array in arrays
    ])


def solution(mesh):
    placed = (
        P("ctx", "head"),
        P("ctx", "head"),
        P("ctx", "head"),
        P("ctx", "head"),
        P("ctx"),
        P(None, "head", "ctx", None),
        P("head"),
    )
    return jax.shard_map(
        on_device,
        mesh=mesh,
        in_specs=placed,
        out_specs=(P("ctx", "head"), P(None, "head", "ctx", None)),
        check_vma=False,
    )
```
